256 devices in a mesh: row: 16 (over x, y), col: 16 (over z, core).
Axes of the slice: x: 4, y: 4, z: 8, core: 2. Of those that a mesh axis runs over, the one named last changes fastest.
Arguments:
- factor: float32 [4, 16, 256, 4, 16, 256], P(None, 'row', None, None, 'col'), as said below
- adjoint: float32 [4, 16, 256, 4, 16, 256], P(None, 'row', None, None, 'col'), may hold values from -6 to 6
- diag_inverse: float32 [2, 256, 256], replicated, as said below
Outputs:
- gradient: float32 [4, 16, 256, 4, 16, 256], P(None, 'row', None, None, 'col')
The draws below stay inside these ranges and needn't reach their ends.
Inputs may be any that keep to these rules, and one draw needn't show every extreme that they name: The diagonal blocks of factor at block indices 32 and 31 are lower triangular with diagonal entries between 1 and 2; diag_inverse[0] and diag_inverse[1] are their inverses. Entries above those blocks' diagonals and above the block diagonal elsewhere are never read. diag_inverse[k] is the inverse of the diagonal block of factor at block index 32 - k.
All inputs are finite; a program needn't handle non-finite values.
Results may differ from the reference program's by a relative error of at most 0.0001.
Values sent between devices are 32-bit elements; how exact they have to be, the bound alone decides.
No kernel may reach another device: no remote copies, remote signals or barrier semaphores. Data moves between devices by JAX's collectives and lax.ppermute only.
A program may use at most 128 MiB of HBM per device.

```python
import math
import jax
import jax.numpy as jnp
from jax import lax

N = 16384
NB = 256
PANEL = 32
LBR = 4
LBC = 4
N_ROW = 16
N_COL = 16


def diagonal_pair(key, panel_step):
    base = jax.random.fold_in(key, 500 + panel_step)
    noise = jax.random.normal(jax.random.fold_in(base, 1), (NB, NB), jnp.float32) * (1.0 / math.sqrt(NB))
    diag_part = jax.random.uniform(jax.random.fold_in(base, 2), (NB,), jnp.float32, 1.0, 2.0)
    row_ids = jnp.arange(NB)[:, None]
    col_ids = jnp.arange(NB)[None, :]
    quadrant = (row_ids >= NB // 2) & (col_ids < NB // 2)
    strict = jnp.where(quadrant, noise, 0.0)
    eye_matrix = jnp.eye(NB, dtype=jnp.float32)
    block = diag_part[:, None] * (eye_matrix - strict)
    inverse = (eye_matrix + strict) / diag_part[None, :]
    return (block, inverse)


def draw_factor(key, part):
    blocks = [diagonal_pair(key, 0)[0], diagonal_pair(key, 1)[0]]
    key = jax.random.fold_in(key, 3)
    scale = 1.0 / math.sqrt(N / 2)
    dense = jax.random.normal(key, (N, N), jnp.float32) * scale
    for panel_step in range(2):
        start = (PANEL - panel_step) * NB
        dense = dense.at[start:start + NB, start:start + NB].set(blocks[panel_step])
    return dense.reshape(LBR, N_ROW, NB, LBC, N_COL, NB)


def draw_diag_inverse(key, part):
    inverses = [diagonal_pair(key, 0)[1], diagonal_pair(key, 1)[1]]
    return jnp.stack(inverses)


def block_levels(key, shape, split, low, largest):
    gain, own = 1.0, jax.random.fold_in(key, 6)
    for axis_at, blocks in split:
        heights = jnp.exp(jax.random.uniform(jax.random.fold_in(own, axis_at), (blocks,), jnp.float32, low / len(split), largest / len(split)))
        gain = gain * jnp.repeat(heights, shape[axis_at] // blocks).reshape([-1 if axis == axis_at else 1 for axis in range(len(shape))])
    return gain


def gaussian(key, shape, deviation, limit, split=(), held_as=jnp.bfloat16):
    result = deviation * jax.random.normal(key, shape, jnp.float32)
    if split:
        result = result * block_levels(key, shape, split, -0.22, 0.18)
    return jnp.clip(result, -limit, limit).astype(held_as)


def setup_inputs(seed: int = 0) -> dict:
    key_list = jax.random.split(jax.random.key(seed), 4)
    factor = draw_factor(jax.random.fold_in(key_list[3], 71), 0)
    adjoint = gaussian(key_list[1], (LBR, N_ROW, NB, LBC, N_COL, NB), 1.0, 6.0, ((1, 16), (4, 16)), jnp.float32)
    diag_inverse = draw_diag_inverse(jax.random.fold_in(key_list[3], 71), 0)
    return dict(factor=factor, adjoint=adjoint, diag_inverse=diag_inverse)


def product(left, right):
    return jnp.dot(left, right, precision=lax.Precision.HIGHEST, preferred_element_type=jnp.float32)


def lower_half(matrix):
    return jnp.tril(matrix) - 0.5 * jnp.diag(jnp.diag(matrix))


def reference(factor, adjoint, diag_inverse):
    lower = factor.reshape(N, N)
    grad = adjoint.reshape(N, N)
    for panel_step in range(2):
        block_index = PANEL - panel_step
        start = block_index * NB
        finish = start + NB
        inverse = diag_inverse[panel_step]
        below = product(grad[finish:, start:finish], inverse)
        row_factor = lower[start:finish, :start]
        grad = grad.at[finish:, :start].set(grad[finish:, :start] - product(below, row_factor))
        dbar = jnp.tril(grad[start:finish, start:finish] - product(below.T, lower[finish:, start:finish]))
        diag_factor = jnp.tril(lower[start:finish, start:finish])
        inner = lower_half(product(diag_factor.T, dbar))
        sym_part = product(product(inverse.T, inner), inverse)
        dbar = lower_half(sym_part + sym_part.T)
        cross = product(below.T, lower[finish:, :start]) + product(dbar + dbar.T, row_factor)
        grad = grad.at[start:finish, :start].set(grad[start:finish, :start] - cross)
        grad = grad.at[finish:, start:finish].set(below)
        grad = grad.at[start:finish, start:finish].set(dbar)
    return grad.reshape(adjoint.shape)
```

```python
import jax
import jax.numpy as jnp
from jax import lax
from jax.sharding import PartitionSpec as P

PANEL = 32


def product(left, right):
    return jnp.dot(left, right, precision=lax.Precision.HIGHEST, preferred_element_type=jnp.float32)


def product_t(left, right):
    return lax.dot_general(
        left, right, (((0,), (0,)), ((), ())), precision=lax.Precision.HIGHEST, preferred_element_type=jnp.float32
    )


def lower_half(matrix):
    rows = lax.broadcasted_iota(jnp.int32, matrix.shape, 0)
    cols = lax.broadcasted_iota(jnp.int32, matrix.shape, 1)
    return jnp.where(rows > cols, matrix, jnp.where(rows == cols, 0.5 * matrix, 0.0))


def two_root_tree(value, axis, index):
    size = lax.axis_size(axis)
    reach = size // 2
    holders = [0]
    while reach >= 2:
        targets = [h + reach for h in holders]
        pairs = list(zip(holders, targets))
        pairs += [(size - 1 - s, size - 1 - t) for s, t in zip(holders, targets)]
        moved = lax.ppermute(value, axis, pairs)
        got = (index % reach == 0) & (index // reach % 2 == 1) | (
            (size - 1 - index) % reach == 0
        ) & ((size - 1 - index) // reach % 2 == 1)
        value = jnp.where(got, moved, value)
        holders = holders + targets
        reach //= 2
    return value


def swap_pairs(value, axis):
    size = lax.axis_size(axis)
    return lax.ppermute(value, axis, [(i, i ^ 1) for i in range(size)])


def both(value, axis, index):
    mine = two_root_tree(value, axis, index)
    other = swap_pairs(mine, axis)
    odd = index % 2 == 1
    return jnp.where(odd, other, mine), jnp.where(odd, mine, other)


def exchange(value, axis):
    size = lax.axis_size(axis)
    parts = value.reshape(size, value.shape[0] // size, value.shape[1])
    return lax.all_to_all(parts, axis, 0, 0)


def reduce_to_parts(value, axis):
    return exchange(value, axis).sum(0)


def gather_parts(part, axis):
    size = lax.axis_size(axis)
    parts = lax.all_to_all(jnp.broadcast_to(part[None], (size,) + part.shape), axis, 0, 0)
    return parts


def per_device(factor, adjoint, diag_inverse):
    my_row = lax.axis_index("row")
    my_col = lax.axis_index("col")
    last_row = lax.axis_size("row") - 1
    last_col = lax.axis_size("col") - 1
    w = adjoint.shape[2]
    lower = factor.reshape(4, w, 4, w)
    grad = adjoint.reshape(4, w, 4, w)
    z0, z1 = diag_inverse[0], diag_inverse[1]
    odd_col = my_col % 2 == 1
    odd_row = my_row % 2 == 1
    live = jnp.where((my_row == 0) & (lax.broadcasted_iota(jnp.int32, (2 * w, 1), 0) < w), 0.0, 1.0)

    slab = jnp.where(odd_col, grad[2:4, :, 1, :], grad[2:4, :, 2, :]).reshape(2 * w, w)
    row_piece = jnp.where(odd_row, lower[1, :, 0:2, :], lower[2, :, 0:2, :]).reshape(w, 2 * w)
    g32, g31 = both(slab, "col", my_col)
    row32, row31 = both(row_piece, "row", my_row)

    sent = lax.ppermute(slab, "col", [(0, last_col)])
    first = jnp.where(my_col == last_col, sent, slab)
    pair = jnp.concatenate([first, slab], axis=1) * live
    factor_slab = jnp.where(odd_col, lower[2:4, :, 1, :], lower[2:4, :, 2, :]).reshape(2 * w, w)
    diag_part = reduce_to_parts(product_t(pair, factor_slab), "row")
    part0, part1 = both(diag_part, "col", my_col)
    diag_sums = gather_parts(jnp.concatenate([part0, part1], axis=1), "row").reshape(2 * w, 2 * w)
    a32 = diag_sums[:w, :w]
    a31 = diag_sums[:w, w:]
    b31 = diag_sums[w:, w:]

    corner = lax.ppermute(grad[1, :, 1, :], "col", [(last_col, 0)])
    at_last = jnp.concatenate([row32[:, w:], row31[:, w:]], axis=0)
    at_first = jnp.concatenate([lower[2, :, 2, :], corner], axis=0)
    small0, small1 = both(jnp.where(odd_col, at_last, at_first), "col", my_col)
    l3232, g3131 = small0[:w], small0[w:]
    l3231, l3131 = small1[:w], small1[w:]
    g3232, g3231 = g32[:w], g31[:w]

    grads = jnp.concatenate([g32, g31], axis=1) * live
    lower_in = lower[2:4, :, 0:2, :].reshape(2 * w, 2 * w)
    sums = reduce_to_parts(product_t(grads, lower_in), "row")
    sums = gather_parts(sums, "row").reshape(2 * w, 2 * w)

    t32 = product_t(z0, a32)
    t31 = product_t(z0, a31)
    inner = lower_half(product_t(jnp.tril(l3232), jnp.tril(g3232 - t32)))
    sym = product(product_t(z0, inner), z0)
    sym0 = sym + sym.T
    below_row = product(g3231 - t31 - product(sym0, l3231), z1)
    below_row = jnp.where(my_row == last_row, lax.ppermute(below_row, "row", [(0, last_row)]), below_row)
    t31b = product_t(z1, b31 - product_t(l3231, t31))
    dbar = jnp.tril(g3131 - t31b - product_t(below_row, l3231))
    inner = lower_half(product_t(jnp.tril(l3131), dbar))
    sym = product(product_t(z1, inner), z1)
    sym1 = sym + sym.T

    below0 = product(g32, z0)
    below1 = product(g31 - product(below0, l3231), z1)
    old = grad[2:4, :, 0:2, :].reshape(2 * w, 2 * w)
    bulk = old - product(
        jnp.concatenate([below0, below1], axis=1), jnp.concatenate([row32, row31], axis=0)
    )
    on_last = my_col == last_col
    on_first = my_col == 0
    bulk = jnp.concatenate([bulk[:, :w], jnp.where(on_last, below1, bulk[:, w:])], axis=1)
    slab_out = jnp.where(on_first, below0, grad[2:4, :, 2, :].reshape(2 * w, w))
    grad = grad.at[2:4, :, 0:3, :].set(jnp.concatenate([bulk, slab_out], axis=1).reshape(2, w, 3, w))

    top = my_row == 0
    coef = jnp.where(
        top,
        jnp.concatenate([z0.T, jnp.zeros_like(z0), sym0, below_row], axis=1),
        jnp.concatenate([-product(z0, product(l3231, z1)).T, z1.T, below_row.T, sym1], axis=1),
    )
    update = product(coef, jnp.concatenate([sums, row32, row31], axis=0))
    at = jnp.where(top, 2, 1)
    before = lax.dynamic_slice(adjoint.reshape(4, w, 4, w), (at, 0, 0, 0), (1, w, 3, w)).reshape(w, 3 * w)
    after = before[:, : 2 * w] - update
    corner_out = jnp.where(top, below_row, lower_half(sym1))
    after = jnp.concatenate(
        [
            after[:, :w],
            jnp.where(on_last, corner_out, after[:, w:]),
            jnp.where(top & on_first, lower_half(sym0), before[:, 2 * w :]),
        ],
        axis=1,
    )
    after = jnp.where(top | (my_row == last_row), after, before)
    grad = lax.dynamic_update_slice(grad, after.reshape(1, w, 3, w), (at, 0, 0, 0))
    return grad.reshape(adjoint.shape)


def solution(mesh):
    placed = (P(None, "row", None, None, "col", None), P(None, "row", None, None, "col", None), P())
    return jax.shard_map(
        per_device,
        mesh=mesh,
        in_specs=placed,
        out_specs=P(None, "row", None, None, "col", None),
        check_vma=False,
    )
```

```python
import functools

import jax
import jax.numpy as jnp
from jax import lax
from jax.experimental import pallas as pl
from jax.experimental.pallas import tpu as pltpu
from jax.sharding import PartitionSpec as P

W = 256
LANES = 128
SUB = 8
ROWS = W * SUB
F32 = jnp.float32
ANY = pl.BlockSpec(memory_space=pl.ANY)
VMEM = pl.BlockSpec(memory_space=pltpu.VMEM)
SMEM = pl.BlockSpec(memory_space=pltpu.SMEM)


def product(left, right):
    return jnp.dot(left, right, precision=lax.Precision.HIGHEST, preferred_element_type=F32)


def product_t(left, right):
    return lax.dot_general(
        left, right, (((0,), (0,)), ((), ())), precision=lax.Precision.HIGHEST, preferred_element_type=F32
    )


def product_nt(left, right):
    return lax.dot_general(
        left, right, (((1,), (1,)), ((), ())), precision=lax.Precision.HIGHEST, preferred_element_type=F32
    )


def masks(size):
    rows = lax.broadcasted_iota(jnp.int32, (size, size), 0)
    cols = lax.broadcasted_iota(jnp.int32, (size, size), 1)
    return rows >= cols, rows == cols


def tril(matrix):
    return jnp.where(masks(matrix.shape[0])[0], matrix, 0.0)


def lower_half(matrix):
    low, diag = masks(matrix.shape[0])
    return jnp.where(diag, 0.5 * matrix, jnp.where(low, matrix, 0.0))


def call(body, out_shape, in_specs, out_specs, scratch, flops, moved, alias=None):
    return pl.pallas_call(
        body,
        out_shape=out_shape,
        in_specs=in_specs,
        out_specs=out_specs,
        scratch_shapes=scratch,
        input_output_aliases=alias or {},
        compiler_params=pltpu.CompilerParams(vmem_limit_bytes=60 * 1024 * 1024),
        cost_estimate=pl.CostEstimate(flops=flops, bytes_accessed=moved, transcendentals=0),
    )


def shape(*dims):
    return jax.ShapeDtypeStruct(dims, F32)


def piece_of(buf, first, rows, k):
    return buf[pl.ds(first * SUB + k, rows, stride=SUB), :]


def entry_kernel(pos, g, l, slab, piece, gbuf, lbuf, sems):
    odd_row = pos[0] % 2
    odd_col = pos[1] % 2
    first = pltpu.make_async_copy(g.at[pl.ds(2 * ROWS, 2 * ROWS)], gbuf, sems.at[0])
    first.start()
    start = pl.multiple_of((2 - odd_row) * ROWS, ROWS)
    second = pltpu.make_async_copy(l.at[pl.ds(start, ROWS)], lbuf, sems.at[1])
    second.start()
    first.wait()
    for odd in range(2):

        @pl.when(odd_col == odd)
        def _():
            for h in range(2):
                slab[:, h * LANES : (h + 1) * LANES] = piece_of(gbuf, 0, 2 * W, 2 * (2 - odd) + h)

    second.wait()
    for k in range(4):
        piece[:, k * LANES : (k + 1) * LANES] = piece_of(lbuf, 0, W, k)


def unpack_kernel(pos, g, l, inside, fslab, corner, ldiag, lbuf, gbuf, sems):
    odd_col = pos[1] % 2
    first = pltpu.make_async_copy(l.at[pl.ds(2 * ROWS, 2 * ROWS)], lbuf, sems.at[0])
    first.start()
    second = pltpu.make_async_copy(g.at[pl.ds(ROWS, ROWS)], gbuf, sems.at[1])
    second.start()
    first.wait()
    for odd in range(2):

        @pl.when(odd_col == odd)
        def _():
            for h in range(2):
                fslab[:, h * LANES : (h + 1) * LANES] = piece_of(lbuf, 0, 2 * W, 2 * (2 - odd) + h)

    for k in range(4):
        inside[:, k * LANES : (k + 1) * LANES] = piece_of(lbuf, 0, 2 * W, k)
    for h in range(2):
        ldiag[:, h * LANES : (h + 1) * LANES] = piece_of(lbuf, 0, W, 4 + h)
    second.wait()
    for h in range(2):
        corner[:, h * LANES : (h + 1) * LANES] = piece_of(gbuf, 0, W, 2 + h)


def pick(pos, axis, mine, other):
    odd = pos[axis] % 2 == 1
    return jnp.where(odd, other, mine), jnp.where(odd, mine, other)


def live_rows(pos, value):
    rows = lax.broadcasted_iota(jnp.int32, value.shape, 0)
    return jnp.where((pos[0] == 0) & (rows < W), 0.0, value)


def diag_kernel(pos, sent, slab, fslab, out):
    right = fslab[...]
    left = jnp.where(pos[1] % 2 == 1, sent[...], slab[...])
    out[:W] = product_t(live_rows(pos, left), right)
    out[W:] = product_t(live_rows(pos, slab[...]), right)


def sums_kernel(pos, mine, other, inside, out):
    g32, g31 = pick(pos, 1, mine[...], other[...])
    right = inside[...]
    out[:W] = product_t(live_rows(pos, g32), right)
    out[W:] = product_t(live_rows(pos, g31), right)


def bulk_kernel(pos, g, gmine, gother, rmine, rother, smine, sother, z, out, gbuf, abuf, b0, b1, sems):
    load = pltpu.make_async_copy(g.at[pl.ds(2 * ROWS, 2 * ROWS)], gbuf, sems.at[0])
    load.start()
    above = pltpu.make_async_copy(g.at[pl.ds(0, 2 * ROWS)], abuf, sems.at[1])
    above.start()
    g32, g31 = pick(pos, 1, gmine[...], gother[...])
    row32, row31 = pick(pos, 0, rmine[...], rother[...])
    l3231 = jnp.where(pos[1] % 2 == 1, smine[:W], sother[:W])
    below0 = product(g32, z[0])
    b0[...] = below0
    below1 = product(g31 - product(below0, l3231), z[1])
    b1[...] = below1
    change = product(below0, row32) + product(below1, row31)
    above.wait()
    rest = pltpu.make_async_copy(abuf, out.at[pl.ds(0, 2 * ROWS)], sems.at[1])
    rest.start()
    load.wait()
    for k in range(4):
        at = pl.ds(k, 2 * W, stride=SUB)
        gbuf[at, :] = gbuf[at, :] - change[:, k * LANES : (k + 1) * LANES]

    @pl.when(pos[1] == 15)
    def _():
        for h in range(2):
            gbuf[pl.ds(2 + h, 2 * W, stride=SUB), :] = b1[:, h * LANES : (h + 1) * LANES]

    @pl.when(pos[1] == 0)
    def _():
        for h in range(2):
            gbuf[pl.ds(4 + h, 2 * W, stride=SUB), :] = b0[:, h * LANES : (h + 1) * LANES]

    store = pltpu.make_async_copy(gbuf, out.at[pl.ds(2 * ROWS, 2 * ROWS)], sems.at[0])
    store.start()
    rest.wait()
    store.wait()


def chain_one_kernel(pos, sums, gmine, gother, smine, sother, z, sym0, below_row):
    @pl.when(pos[0] == 0)
    def _():
        z0, z1 = z[0], z[1]
        g3232, g3231 = pick(pos, 1, gmine[:W], gother[:W])
        small0, small1 = pick(pos, 1, smine[:W], sother[:W])
        t32 = product_t(z0, sums[:W, :W])
        t31 = product_t(z0, sums[:W, W:])
        inner = lower_half(product_t(tril(small0), tril(g3232 - t32)))
        sym = product(product_t(z0, inner), z0)
        sym = sym + sym.T
        sym0[...] = sym
        below_row[...] = product(g3231 - t31 - product(sym, small1), z1)

    @pl.when(pos[0] != 0)
    def _():
        sym0[...] = jnp.zeros_like(sym0)
        below_row[...] = jnp.zeros_like(below_row)


def chain_two_kernel(pos, sums, smine, sother, below_row, z, sym1, mix):
    @pl.when(pos[0] == 15)
    def _():
        z0, z1 = z[0], z[1]
        small0, small1 = pick(pos, 1, smine[...], sother[...])
        l3231, l3131, g3131 = small1[:W], small1[W:], small0[W:]
        t31 = product_t(z0, sums[:W, W:])
        t31b = product_t(z1, sums[W:, W:] - product_t(l3231, t31))
        dbar = tril(g3131 - t31b - product_t(below_row[...], l3231))
        inner = lower_half(product_t(tril(l3131), dbar))
        sym = product(product_t(z1, inner), z1)
        sym1[...] = sym + sym.T
        mix[...] = product(z0, product(l3231, z1))

    @pl.when(pos[0] != 15)
    def _():
        sym1[...] = jnp.zeros_like(sym1)
        mix[...] = jnp.zeros_like(mix)


def finish_kernel(pos, g, sums, rmine, rother, sym0, b_here, b_sent, sym1, mix, z, done, out, gbuf, sem):
    def panel_row(first, update, corner, extra):
        load = pltpu.make_async_copy(g.at[pl.ds(first * ROWS, ROWS)], gbuf, sem)
        load.start()
        change = update()
        load.wait()
        for k in range(4):
            at = pl.ds(k, W, stride=SUB)
            gbuf[at, :] = gbuf[at, :] - change[:, k * LANES : (k + 1) * LANES]

        @pl.when(pos[1] == 15)
        def _():
            for h in range(2):
                gbuf[pl.ds(2 + h, W, stride=SUB), :] = corner()[:, h * LANES : (h + 1) * LANES]

        if extra is not None:

            @pl.when(pos[1] == 0)
            def _():
                for h in range(2):
                    gbuf[pl.ds(4 + h, W, stride=SUB), :] = extra()[:, h * LANES : (h + 1) * LANES]

        store = pltpu.make_async_copy(gbuf, out.at[pl.ds(first * ROWS, ROWS)], sem)
        store.start()
        store.wait()

    @pl.when(pos[0] == 0)
    def _():
        def update():
            row32, row31 = pick(pos, 0, rmine[...], rother[...])
            return (
                product_t(z[0], sums[:W]) + product(sym0[...], row32) + product(b_here[...], row31)
            )

        panel_row(2, update, lambda: b_here[...], lambda: lower_half(sym0[...]))

    @pl.when(pos[0] == 15)
    def _():
        def update():
            row32, row31 = pick(pos, 0, rmine[...], rother[...])
            return (
                product_t(z[1], sums[W:])
                - product_t(mix[...], sums[:W])
                + product_t(b_sent[...], row32)
                + product(sym1[...], row31)
            )

        panel_row(1, update, lambda: lower_half(sym1[...]), None)


def tree_step(value, axis, step):
    size = lax.axis_size(axis)
    reach = size >> (step + 1)
    pairs = [(h, h + reach) for h in range(0, size, 2 * reach)]
    pairs = pairs + [(size - 1 - s, size - 1 - t) for s, t in pairs]
    moved = lax.ppermute(value, axis, pairs)
    index = lax.axis_index(axis)
    got = functools.reduce(jnp.logical_or, [index == t for _, t in pairs])
    return jnp.where(got, moved, value)


def tree(value, axis):
    for step in range(3):
        value = tree_step(value, axis, step)
    return value


def after(value, *others):
    return lax.optimization_barrier((value, *others))[0]


def swap(value, axis):
    size = lax.axis_size(axis)
    return lax.ppermute(value, axis, [(i, i ^ 1) for i in range(size)])


def exchange(value, axis):
    size = lax.axis_size(axis)
    parts = value.reshape(size, value.shape[0] // size, value.shape[1])
    return lax.all_to_all(parts, axis, 0, 0)


def gather_parts(part, axis):
    size = lax.axis_size(axis)
    parts = jnp.broadcast_to(part[None], (size,) + part.shape)
    parts = lax.all_to_all(parts, axis, 0, 0)
    return parts.reshape(size * part.shape[0], part.shape[1])


def per_device(factor, adjoint, diag_inverse):
    my_row = lax.axis_index("row")
    my_col = lax.axis_index("col")
    pos = jnp.stack([my_row, my_col]).astype(jnp.int32)
    odd_col = my_col % 2 == 1
    g = adjoint.reshape(4 * ROWS, LANES)
    l = factor.reshape(4 * ROWS, LANES)
    z = diag_inverse
    dma = pltpu.SemaphoreType.DMA
    block = W * W * 4

    slab, piece = call(
        entry_kernel,
        (shape(2 * W, W), shape(W, 2 * W)),
        [SMEM, ANY, ANY],
        (VMEM, VMEM),
        [pltpu.VMEM((2 * ROWS, LANES), F32), pltpu.VMEM((ROWS, LANES), F32), dma((2,))],
        0,
        16 * block,
    )(pos, g, l)
    sent = lax.ppermute(slab, "col", [(0, 15)])
    gmine = tree_step(slab, "col", 0)
    rmine = tree_step(piece, "row", 0)
    gmine, rmine = after(gmine, rmine), after(rmine, gmine)
    inside, fslab, corner, ldiag = call(
        unpack_kernel,
        (shape(2 * W, 2 * W), shape(2 * W, W), shape(W, W), shape(W, W)),
        [SMEM, ANY, ANY],
        (VMEM,) * 4,
        [pltpu.VMEM((2 * ROWS, LANES), F32), pltpu.VMEM((ROWS, LANES), F32), dma((2,))],
        0,
        20 * block,
    )(pos, g, l)

    gmine2 = tree_step(gmine, "col", 1)
    rmine2 = tree_step(rmine, "row", 1)

    partial = call(
        diag_kernel, shape(2 * W, W), [SMEM] + [VMEM] * 3, VMEM, [], 8 * W**3, 8 * block
    )(pos, sent, slab, fslab)
    diag_parts = exchange(after(partial, gmine2, rmine2), "row")
    gmine, rmine = after(gmine2, rmine2, partial), after(rmine2, gmine2, partial)
    gmine, rmine = tree_step(gmine, "col", 2), tree_step(rmine, "row", 2)
    gmine, rmine = after(gmine, rmine), after(rmine, gmine)
    gother, rother = swap(gmine, "col"), swap(rmine, "row")
    diag_mine = tree(after(diag_parts, gother).sum(0), "col")
    diag_other = swap(diag_mine, "col")
    diag_cols = jnp.where(
        odd_col,
        jnp.concatenate([diag_other, diag_mine], axis=1),
        jnp.concatenate([diag_mine, diag_other], axis=1),
    )
    diag_sums = gather_parts(diag_cols, "row")

    sums = call(
        sums_kernel, shape(2 * W, 2 * W), [SMEM] + [VMEM] * 3, VMEM, [], 16 * W**3, 12 * block
    )(pos, gmine, gother, inside)
    sums = gather_parts(exchange(sums, "row").sum(0), "row")

    corner = lax.ppermute(corner, "col", [(15, 0)])
    at_first = jnp.concatenate([ldiag, corner], axis=0)
    odd_row = my_row % 2 == 1
    row32 = jnp.where(odd_row, rother[:, W:], rmine[:, W:])
    row31 = jnp.where(odd_row, rmine[:, W:], rother[:, W:])
    at_last = jnp.concatenate([row32, row31], axis=0)
    smine = tree(jnp.where(odd_col, at_last, at_first), "col")
    sother = swap(smine, "col")

    out = call(
        bulk_kernel,
        shape(4 * ROWS, LANES),
        [SMEM, ANY] + [VMEM] * 7,
        ANY,
        [
            pltpu.VMEM((2 * ROWS, LANES), F32),
            pltpu.VMEM((2 * ROWS, LANES), F32),
            pltpu.VMEM((2 * W, W), F32),
            pltpu.VMEM((2 * W, W), F32),
            dma((2,)),
        ],
        30 * W**3,
        40 * block,
    )(pos, g, gmine, gother, rmine, rother, smine, sother, z)

    sym0, below_row = call(
        chain_one_kernel, (shape(W, W),) * 2, [SMEM] + [VMEM] * 6, (VMEM,) * 2, [], 16 * W**3, 12 * block
    )(pos, diag_sums, gmine, gother, smine, sother, z)
    below_sent = lax.ppermute(below_row, "row", [(0, 15)])
    sym1, mix = call(
        chain_two_kernel, (shape(W, W),) * 2, [SMEM] + [VMEM] * 5, (VMEM,) * 2, [], 16 * W**3, 12 * block
    )(pos, diag_sums, smine, sother, below_sent, z)
    out = call(
        finish_kernel,
        shape(4 * ROWS, LANES),
        [SMEM, ANY] + [VMEM] * 9 + [ANY],
        ANY,
        [pltpu.VMEM((ROWS, LANES), F32), dma],
        16 * W**3,
        16 * block,
        alias={11: 0},
    )(pos, g, sums, rmine, rother, sym0, below_row, below_sent, sym1, mix, z, out)
    return out.reshape(adjoint.shape)


def solution(mesh):
    placed = (P(None, "row", None, None, "col", None), P(None, "row", None, None, "col", None), P())
    return jax.shard_map(
        per_device,
        mesh=mesh,
        in_specs=placed,
        out_specs=P(None, "row", None, None, "col", None),
        check_vma=False,
    )
```

```python
import functools

import jax
import jax.numpy as jnp
from jax import lax
from jax.experimental import pallas as pl
from jax.experimental.pallas import tpu as pltpu
from jax.sharding import PartitionSpec as P

W = 256
LANES = 128
SUB = 8
ROWS = W * SUB
F32 = jnp.float32
DIAG_HINT = 20 * 10**9
MAIN_HINT = 100 * 10**9
CHAIN_HINT = 40 * 10**9
STEP_HINT = 25 * 10**9
LIGHT = 1000
SUMS_HINT = 3 * 10**8
ANY = pl.BlockSpec(memory_space=pl.ANY)
HBM = pl.BlockSpec(memory_space=pltpu.HBM)
VMEM = pl.BlockSpec(memory_space=pltpu.VMEM)
SMEM = pl.BlockSpec(memory_space=pltpu.SMEM)


def product(left, right):
    return jnp.dot(left, right, precision=lax.Precision.HIGHEST, preferred_element_type=F32)


def product_t(left, right):
    return lax.dot_general(
        left, right, (((0,), (0,)), ((), ())), precision=lax.Precision.HIGHEST, preferred_element_type=F32
    )


def product_nt(left, right):
    return lax.dot_general(
        left, right, (((1,), (1,)), ((), ())), precision=lax.Precision.HIGHEST, preferred_element_type=F32
    )


def masks(size):
    rows = lax.broadcasted_iota(jnp.int32, (size, size), 0)
    cols = lax.broadcasted_iota(jnp.int32, (size, size), 1)
    return rows >= cols, rows == cols


def tril(matrix):
    return jnp.where(masks(matrix.shape[0])[0], matrix, 0.0)


def lower_half(matrix):
    low, diag = masks(matrix.shape[0])
    return jnp.where(diag, 0.5 * matrix, jnp.where(low, matrix, 0.0))


def call(body, out_shape, in_specs, out_specs, scratch, flops, moved, alias=None, vmem=20):
    return pl.pallas_call(
        body,
        out_shape=out_shape,
        in_specs=in_specs,
        out_specs=out_specs,
        scratch_shapes=scratch,
        input_output_aliases=alias or {},
        compiler_params=pltpu.CompilerParams(vmem_limit_bytes=vmem * 1024 * 1024),
        cost_estimate=pl.CostEstimate(flops=flops, bytes_accessed=moved, transcendentals=0),
    )


def shape(*dims):
    return jax.ShapeDtypeStruct(dims, F32)


def piece_of(buf, first, rows, k):
    return buf[pl.ds(first * SUB + k, rows, stride=SUB), :]


def entry_kernel(pos, g, l, slab, piece, corner, gbuf, lbuf, cbuf, sems):
    odd_row = pos[2]
    odd_col = pos[3]
    first = pltpu.make_async_copy(g.at[pl.ds(2 * ROWS, 2 * ROWS)], gbuf, sems.at[0])
    first.start()
    start = pl.multiple_of((2 - odd_row) * ROWS, ROWS)
    second = pltpu.make_async_copy(l.at[pl.ds(start, ROWS)], lbuf, sems.at[1])
    second.start()
    third = pltpu.make_async_copy(g.at[pl.ds(ROWS, ROWS)], cbuf, sems.at[2])
    third.start()
    first.wait()
    for odd in range(2):

        @pl.when(odd_col == odd)
        def _():
            for h in range(2):
                slab[:, h * LANES : (h + 1) * LANES] = piece_of(gbuf, 0, 2 * W, 2 * (2 - odd) + h)

    second.wait()
    for k in range(4):
        piece[:, k * LANES : (k + 1) * LANES] = piece_of(lbuf, 0, W, k)
    third.wait()
    for h in range(2):
        corner[:, h * LANES : (h + 1) * LANES] = piece_of(cbuf, 0, W, 2 + h)


def unpack_kernel(pos, l, slab, corner, inside, fslab, own, lbuf, sem):
    odd_col = pos[3]
    first = pltpu.make_async_copy(l.at[pl.ds(2 * ROWS, 2 * ROWS)], lbuf, sem)
    first.start()
    first.wait()
    for odd in range(2):

        @pl.when(odd_col == odd)
        def _():
            for h in range(2):
                fslab[:, h * LANES : (h + 1) * LANES] = piece_of(lbuf, 0, 2 * W, 2 * (2 - odd) + h)

    for k in range(4):
        inside[:, k * LANES : (k + 1) * LANES] = piece_of(lbuf, 0, 2 * W, k)
    for h in range(2):
        own[W:, h * LANES : (h + 1) * LANES] = piece_of(lbuf, 0, W, 4 + h)
    own[:W] = jnp.where(pos[0] == 15, corner[...], slab[:W])


def pick(pos, axis, mine, other):
    odd = pos[2 + axis] == 1
    return jnp.where(odd, other, mine), jnp.where(odd, mine, other)


def live_rows(pos, value):
    rows = lax.broadcasted_iota(jnp.int32, value.shape, 0)
    return jnp.where((pos[0] == 0) & (rows < W), 0.0, value)


def diag_kernel(pos, sent, slab, fslab, piece, out):
    right = fslab[...]
    left = jnp.where(pos[3] == 1, sent[...], slab[...])
    for half, value in enumerate((left, slab[...])):
        result = product_t(live_rows(pos, value), right)
        for j in range(8):
            out[8 * half + j, :32] = result[32 * j : 32 * j + 32]
    for j in range(16):
        for h in range(2):
            out[j, 32 + 16 * h : 48 + 16 * h] = piece[16 * j : 16 * j + 16, h * W : (h + 1) * W]


def first_parts_kernel(parts, out, chunk):
    total = parts[0, :32]
    for i in range(1, 16):
        total = total + parts[i, :32]
    for h in range(2):
        lanes = slice(h * W, (h + 1) * W)
        for j in range(16):
            out[j, :16, lanes] = total[16 * h : 16 * h + 16]
            out[j, 16:, lanes] = parts[0, 48 + 8 * h : 56 + 8 * h]
        for k, source in enumerate((0, 15)):
            chunk[16 * k : 16 * k + 16, lanes] = parts[source, 32 + 16 * h : 48 + 16 * h]


def panel_row(panels, which):
    return panels[:, 32 + 16 * which : 48 + 16 * which, :].reshape(W, 2 * W)


def diag_sum(parts, half):
    return jnp.concatenate(
        [parts[8 * half + j, :16, h * W : (h + 1) * W] for j in range(8) for h in range(2)], axis=0
    )


def l3231_of(parts):
    return jnp.concatenate(
        [parts[j, 16:, h * W : (h + 1) * W] for j in range(16) for h in range(2)], axis=0
    )


def sums_kernel(pos, mine, other, inside, chunk, out):
    right = inside[...]
    for half, value in enumerate(pick(pos, 1, mine[...], other[...])):
        result = product_t(live_rows(pos, value), right)
        for j in range(8):
            out[8 * half + j, :32] = result[32 * j : 32 * j + 32]
    for j in range(16):
        out[j, 32:] = chunk[...]


def second_parts_kernel(parts, out):
    total = parts[0, :32]
    for i in range(1, 16):
        total = total + parts[i, :32]
    for i in range(16):
        out[i] = total


def bulk_kernel(pos, g, gmine, gother, panels, smine, sother, z, out, gbuf, abuf, b0, b1, sems):
    load = pltpu.make_async_copy(g.at[pl.ds(2 * ROWS, 2 * ROWS)], gbuf, sems.at[0])
    load.start()
    above = pltpu.make_async_copy(g.at[pl.ds(0, 2 * ROWS)], abuf, sems.at[1])
    above.start()
    g32, g31 = pick(pos, 1, gmine[...], gother[...])
    l3231 = jnp.where(pos[3] == 1, smine[W:], sother[W:])
    below0 = product(g32, z[0])
    b0[...] = below0
    below1 = product(g31 - product(below0, l3231), z[1])
    b1[...] = below1
    change = product(below0, panel_row(panels, 0)) + product(below1, panel_row(panels, 1))
    above.wait()
    rest = pltpu.make_async_copy(abuf, out.at[pl.ds(0, 2 * ROWS)], sems.at[1])
    rest.start()
    load.wait()
    for k in range(4):
        at = pl.ds(k, 2 * W, stride=SUB)
        gbuf[at, :] = gbuf[at, :] - change[:, k * LANES : (k + 1) * LANES]

    @pl.when(pos[1] == 15)
    def _():
        for h in range(2):
            gbuf[pl.ds(2 + h, 2 * W, stride=SUB), :] = b1[:, h * LANES : (h + 1) * LANES]

    @pl.when(pos[1] == 0)
    def _():
        for h in range(2):
            gbuf[pl.ds(4 + h, 2 * W, stride=SUB), :] = b0[:, h * LANES : (h + 1) * LANES]

    store = pltpu.make_async_copy(gbuf, out.at[pl.ds(2 * ROWS, 2 * ROWS)], sems.at[0])
    store.start()
    rest.wait()
    store.wait()


def corner_kernel(pos, parts, own, sent, z, out):
    row, col = pos[0], pos[1]
    out[W:] = l3231_of(parts)

    @pl.when((row == 0) & (col == 0))
    def _():
        dbar = tril(own[:W] - product_t(z[0], diag_sum(parts, 0)))
        inner = lower_half(product_t(tril(own[W:]), dbar))
        sym = product(product_t(z[0], inner), z[0])
        out[:W] = sym + sym.T

    @pl.when((row == 0) & (col == 15))
    def _():
        out[:W] = own[:W] - product_t(z[0], diag_sum(parts, 0))

    @pl.when((row == 15) & (col == 15))
    def _():
        t31 = product_t(z[0], diag_sum(parts, 0))
        out[:W] = own[:W] - product_t(z[1], diag_sum(parts, 1) - product_t(out[W:], t31))

    @pl.when(((row != 0) & (row != 15)) | ((col != 0) & (col != 15)) | ((row == 15) & (col == 0)))
    def _():
        out[:W] = sent[...]


def below_kernel(pos, smine, sother, z, out):
    @pl.when(pos[0] == 0)
    def _():
        small0, small1 = pick(pos, 1, smine[...], sother[...])
        out[...] = product(small1[:W] - product(small0[:W], small1[W:]), z[1])

    @pl.when(pos[0] != 0)
    def _():
        out[...] = jnp.zeros_like(out)


def rows_kernel(pos, g, sums, panels, smine, sother, b_here, b_sent, z, done, out, gbuf, sem):
    small0, small1 = pick(pos, 1, smine[...], sother[...])

    def finished_row(first, update, corner, extra):
        load = pltpu.make_async_copy(g.at[pl.ds(first * ROWS, ROWS)], gbuf, sem)
        load.start()
        change = update()
        load.wait()
        for k in range(4):
            at = pl.ds(k, W, stride=SUB)
            gbuf[at, :] = gbuf[at, :] - change[:, k * LANES : (k + 1) * LANES]

        @pl.when(pos[1] == 15)
        def _():
            for h in range(2):
                gbuf[pl.ds(2 + h, W, stride=SUB), :] = corner[:, h * LANES : (h + 1) * LANES]

        if extra is not None:

            @pl.when(pos[1] == 0)
            def _():
                for h in range(2):
                    gbuf[pl.ds(4 + h, W, stride=SUB), :] = extra[:, h * LANES : (h + 1) * LANES]

        store = pltpu.make_async_copy(gbuf, out.at[pl.ds(first * ROWS, ROWS)], sem)
        store.start()
        store.wait()

    @pl.when(pos[0] == 0)
    def _():
        sym0 = small0[:W]

        def update():
            return (
                product_t(z[0], sums[:W])
                + product(sym0, panel_row(panels, 0))
                + product(b_here[...], panel_row(panels, 1))
            )

        finished_row(2, update, b_here[...], lower_half(sym0))

    @pl.when(pos[0] == 15)
    def _():
        l3131, l3231 = small0[:W], small1[W:]
        dbar = tril(small1[:W] - product_t(b_sent[...], l3231))
        inner = lower_half(product_t(tril(l3131), dbar))
        sym1 = product(product_t(z[1], inner), z[1])
        sym1 = sym1 + sym1.T

        def update():
            mix = product(z[0], product(l3231, z[1]))
            return (
                product_t(z[1], sums[W:])
                - product_t(mix, sums[:W])
                + product_t(b_sent[...], panel_row(panels, 0))
                + product(sym1, panel_row(panels, 1))
            )

        finished_row(1, update, lower_half(sym1), None)


RING = [[(0, 7)], [(0, 2), (7, 5)], [(0, 1), (7, 6), (5, 4), (2, 3)]]


def choose_kernel(pos, moved, kept, out, *, targets):
    got = functools.reduce(jnp.logical_or, [pos[1] == t for t in targets])

    @pl.when(got)
    def _():
        out[...] = moved[...]

    @pl.when(jnp.logical_not(got))
    def _():
        out[...] = kept[...]


def tree_step(pos, value, step, weight):
    pairs = [(2 * s, 2 * t) for s, t in RING[step]]
    pairs = pairs + [(15 - s, 15 - t) for s, t in pairs]
    moved = lax.ppermute(value, "col", pairs)
    kernel = functools.partial(choose_kernel, targets=[t for _, t in pairs])
    return call(kernel, shape(*value.shape), [SMEM] + [VMEM] * 2, VMEM, [], weight, 4 * value.size)(pos, moved, value)


def flipped(value, axis, flip):
    return lax.ppermute(value, axis, [(i, i ^ flip) for i in range(lax.axis_size(axis))])


def after(value, *others):
    return lax.optimization_barrier((value, *others))[0]


def exchange(parts):
    return lax.all_to_all(parts, "row", 0, 0)


def per_device(factor, adjoint, diag_inverse):
    my_row = lax.axis_index("row")
    my_col = lax.axis_index("col")
    pos = jnp.stack([my_row, my_col, my_row // 8, my_col % 2]).astype(jnp.int32)
    g = adjoint.reshape(4 * ROWS, LANES)
    l = factor.reshape(4 * ROWS, LANES)
    z = diag_inverse
    dma = pltpu.SemaphoreType.DMA
    block = W * W * 4

    slab, piece, corner = call(
        entry_kernel,
        (shape(2 * W, W), shape(W, 2 * W), shape(W, W)),
        [SMEM, HBM, HBM],
        (VMEM,) * 3,
        [
            pltpu.VMEM((2 * ROWS, LANES), F32),
            pltpu.VMEM((ROWS, LANES), F32),
            pltpu.VMEM((ROWS, LANES), F32),
            dma((3,)),
        ],
        0,
        16 * block,
        vmem=60,
    )(pos, g, l)
    gmine = tree_step(pos, slab, 0, LIGHT)
    inside, fslab, own = call(
        unpack_kernel,
        (shape(2 * W, 2 * W), shape(2 * W, W), shape(2 * W, W)),
        [SMEM, HBM, VMEM, VMEM],
        (VMEM,) * 3,
        [pltpu.VMEM((2 * ROWS, LANES), F32), dma],
        0,
        16 * block,
    )(pos, l, slab, corner)
    gmine = after(gmine, fslab)
    sent = lax.ppermute(gmine, "col", [(14, 15)])
    gmine = tree_step(pos, gmine, 1, STEP_HINT)

    partial = call(
        diag_kernel, shape(16, 64, W), [SMEM] + [VMEM] * 4, VMEM, [], 8 * W**3, 12 * block
    )(pos, sent, slab, fslab, piece)
    parts = exchange(partial)
    gmine = after(gmine, partial)
    spread, chunk = call(
        first_parts_kernel,
        (shape(16, 24, 2 * W), shape(32, 2 * W)),
        [VMEM],
        (VMEM,) * 2,
        [],
        DIAG_HINT,
        10 * block,
    )(after(parts, gmine))
    gmine = tree_step(pos, gmine, 2, STEP_HINT)
    gother = flipped(after(gmine, spread), "col", 1)
    spread = exchange(spread)

    partial = call(
        sums_kernel, shape(16, 64, 2 * W), [SMEM] + [VMEM] * 4, VMEM, [], SUMS_HINT, 20 * block
    )(pos, gmine, gother, inside, chunk)
    panels = exchange(after(partial, spread))

    sent = lax.ppermute(after(piece[:, W:], gmine), "col", [(15, 0)])
    smine = call(
        corner_kernel, shape(2 * W, W), [SMEM] + [VMEM] * 4, VMEM, [], CHAIN_HINT, 12 * block
    )(pos, after(spread, partial), own, sent, z)
    for step in range(3):
        smine = tree_step(pos, smine, step, LIGHT)
    sother = flipped(smine, "col", 1)

    sums = call(
        second_parts_kernel, shape(16, 32, 2 * W), [VMEM], VMEM, [], MAIN_HINT, 8 * block
    )(panels)
    sums = exchange(sums).reshape(2 * W, 2 * W)

    out = call(
        bulk_kernel,
        shape(4 * ROWS, LANES),
        [SMEM, HBM] + [VMEM] * 6,
        HBM,
        [
            pltpu.VMEM((2 * ROWS, LANES), F32),
            pltpu.VMEM((2 * ROWS, LANES), F32),
            pltpu.VMEM((2 * W, W), F32),
            pltpu.VMEM((2 * W, W), F32),
            dma((2,)),
        ],
        30 * W**3,
        40 * block,
        vmem=57,
    )(pos, g, gmine, gother, panels, smine, sother, z)

    below_row = call(
        below_kernel, shape(W, W), [SMEM] + [VMEM] * 3, VMEM, [], 4 * W**3, 8 * block
    )(pos, smine, sother, z)
    below_sent = lax.ppermute(below_row, "row", [(0, 15)])
    out = call(
        rows_kernel,
        shape(4 * ROWS, LANES),
        [SMEM, HBM] + [VMEM] * 7 + [HBM],
        HBM,
        [pltpu.VMEM((ROWS, LANES), F32), dma],
        LIGHT,
        LIGHT,
        alias={9: 0},
        vmem=57,
    )(pos, g, sums, panels, smine, sother, below_row, below_sent, z, out)
    return out.reshape(adjoint.shape)


def solution(mesh):
    placed = (P(None, "row", None, None, "col", None), P(None, "row", None, None, "col", None), P())
    return jax.shard_map(
        per_device,
        mesh=mesh,
        in_specs=placed,
        out_specs=P(None, "row", None, None, "col", None),
        check_vma=False,
    )
```

```python
import functools

import jax
import jax.numpy as jnp
from jax import lax
from jax.experimental import pallas as pl
from jax.experimental.pallas import tpu as pltpu
from jax.sharding import PartitionSpec as P

W = 256
LANES = 128
SUB = 8
ROWS = W * SUB
F32 = jnp.float32
DIAG_HINT = 20 * 10**9
MAIN_HINT = 100 * 10**9
CHAIN_HINT = 40 * 10**9
STEP_HINT = 25 * 10**9
LIGHT = 1000
SUMS_HINT = 3 * 10**8
ANY = pl.BlockSpec(memory_space=pl.ANY)
HBM = pl.BlockSpec(memory_space=pltpu.HBM)
VMEM = pl.BlockSpec(memory_space=pltpu.VMEM)
SMEM = pl.BlockSpec(memory_space=pltpu.SMEM)


def product(left, right):
    return jnp.dot(left, right, precision=lax.Precision.HIGHEST, preferred_element_type=F32)


def product_t(left, right):
    return lax.dot_general(
        left, right, (((0,), (0,)), ((), ())), precision=lax.Precision.HIGHEST, preferred_element_type=F32
    )


def product_nt(left, right):
    return lax.dot_general(
        left, right, (((1,), (1,)), ((), ())), precision=lax.Precision.HIGHEST, preferred_element_type=F32
    )


def masks(size):
    rows = lax.broadcasted_iota(jnp.int32, (size, size), 0)
    cols = lax.broadcasted_iota(jnp.int32, (size, size), 1)
    return rows >= cols, rows == cols


def tril(matrix):
    return jnp.where(masks(matrix.shape[0])[0], matrix, 0.0)


def lower_half(matrix):
    low, diag = masks(matrix.shape[0])
    return jnp.where(diag, 0.5 * matrix, jnp.where(low, matrix, 0.0))


def call(body, out_shape, in_specs, out_specs, scratch, flops, moved, alias=None, vmem=20):
    return pl.pallas_call(
        body,
        out_shape=out_shape,
        in_specs=in_specs,
        out_specs=out_specs,
        scratch_shapes=scratch,
        input_output_aliases=alias or {},
        compiler_params=pltpu.CompilerParams(vmem_limit_bytes=vmem * 1024 * 1024),
        cost_estimate=pl.CostEstimate(flops=flops, bytes_accessed=moved, transcendentals=0),
    )


def shape(*dims):
    return jax.ShapeDtypeStruct(dims, F32)


def piece_of(buf, first, rows, k):
    return buf[pl.ds(first * SUB + k, rows, stride=SUB), :]


def entry_kernel(g, slab, gbuf, sem):
    load = pltpu.make_async_copy(g.at[pl.ds(2 * ROWS, 2 * ROWS)], gbuf, sem)
    load.start()
    odd_col = lax.axis_index("col") % 2
    load.wait()
    for odd in range(2):

        @pl.when(odd_col == odd)
        def _():
            for h in range(2):
                slab[:, h * LANES : (h + 1) * LANES] = piece_of(gbuf, 0, 2 * W, 2 * (2 - odd) + h)


def unpack_kernel(pos, g, l, slab, inside, fslab, piece, own, lbuf, pbuf, gbuf, sems):
    odd_col = pos[3]
    first = pltpu.make_async_copy(l.at[pl.ds(2 * ROWS, 2 * ROWS)], lbuf, sems.at[0])
    first.start()
    start = pl.multiple_of((2 - pos[2]) * ROWS, ROWS)
    second = pltpu.make_async_copy(l.at[pl.ds(start, ROWS)], pbuf, sems.at[1])
    second.start()
    third = pltpu.make_async_copy(g.at[pl.ds(ROWS, ROWS)], gbuf, sems.at[2])
    third.start()
    first.wait()
    for odd in range(2):

        @pl.when(odd_col == odd)
        def _():
            for h in range(2):
                fslab[:, h * LANES : (h + 1) * LANES] = piece_of(lbuf, 0, 2 * W, 2 * (2 - odd) + h)

    for k in range(4):
        inside[:, k * LANES : (k + 1) * LANES] = piece_of(lbuf, 0, 2 * W, k)
    for h in range(2):
        own[W:, h * LANES : (h + 1) * LANES] = piece_of(lbuf, 0, W, 4 + h)
    second.wait()
    for k in range(4):
        piece[:, k * LANES : (k + 1) * LANES] = piece_of(pbuf, 0, W, k)
    third.wait()

    @pl.when(pos[0] == 15)
    def _():
        for h in range(2):
            own[:W, h * LANES : (h + 1) * LANES] = piece_of(gbuf, 0, W, 2 + h)

    @pl.when(pos[0] != 15)
    def _():
        own[:W] = slab[:W]


def pick(pos, axis, mine, other):
    odd = pos[2 + axis] == 1
    return jnp.where(odd, other, mine), jnp.where(odd, mine, other)


def live_rows(pos, value):
    rows = lax.broadcasted_iota(jnp.int32, value.shape, 0)
    return jnp.where((pos[0] == 0) & (rows < W), 0.0, value)


def diag_kernel(pos, sent, slab, fslab, piece, out):
    right = fslab[...]
    left = jnp.where(pos[3] == 1, sent[...], slab[...])
    for half, value in enumerate((left, slab[...])):
        result = product_t(live_rows(pos, value), right)
        for j in range(8):
            out[8 * half + j, :32] = result[32 * j : 32 * j + 32]
    for j in range(16):
        for h in range(2):
            out[j, 32 + 16 * h : 48 + 16 * h] = piece[16 * j : 16 * j + 16, h * W : (h + 1) * W]


def first_parts_kernel(parts, out, chunk):
    total = parts[0, :32]
    for i in range(1, 16):
        total = total + parts[i, :32]
    for h in range(2):
        lanes = slice(h * W, (h + 1) * W)
        for j in range(16):
            out[j, :16, lanes] = total[16 * h : 16 * h + 16]
            out[j, 16:, lanes] = parts[0, 48 + 8 * h : 56 + 8 * h]
        for k, source in enumerate((0, 15)):
            chunk[16 * k : 16 * k + 16, lanes] = parts[source, 32 + 16 * h : 48 + 16 * h]


def panel_row(panels, which):
    return panels[:, 32 + 16 * which : 48 + 16 * which, :].reshape(W, 2 * W)


def diag_sum(parts, half):
    return jnp.concatenate(
        [parts[8 * half + j, :16, h * W : (h + 1) * W] for j in range(8) for h in range(2)], axis=0
    )


def l3231_of(parts):
    return jnp.concatenate(
        [parts[j, 16:, h * W : (h + 1) * W] for j in range(16) for h in range(2)], axis=0
    )


def sums_kernel(pos, mine, other, inside, chunk, out):
    right = inside[...]
    for half, value in enumerate(pick(pos, 1, mine[...], other[...])):
        result = product_t(live_rows(pos, value), right)
        for j in range(8):
            out[8 * half + j, :32] = result[32 * j : 32 * j + 32]
    for j in range(16):
        out[j, 32:] = chunk[...]


def second_parts_kernel(parts, out):
    total = parts[0, :32]
    for i in range(1, 16):
        total = total + parts[i, :32]
    for i in range(16):
        out[i] = total


def bulk_kernel(pos, g, gmine, gother, panels, smine, sother, z, out, gbuf, abuf, b0, b1, sems):
    load = pltpu.make_async_copy(g.at[pl.ds(2 * ROWS, 2 * ROWS)], gbuf, sems.at[0])
    load.start()
    above = pltpu.make_async_copy(g.at[pl.ds(0, 2 * ROWS)], abuf, sems.at[1])
    above.start()
    g32, g31 = pick(pos, 1, gmine[...], gother[...])
    l3231 = jnp.where(pos[3] == 1, smine[W:], sother[W:])
    below0 = product(g32, z[0])
    b0[...] = below0
    below1 = product(g31 - product(below0, l3231), z[1])
    b1[...] = below1
    change = product(below0, panel_row(panels, 0)) + product(below1, panel_row(panels, 1))
    above.wait()
    rest = pltpu.make_async_copy(abuf, out.at[pl.ds(0, 2 * ROWS)], sems.at[1])
    rest.start()
    load.wait()
    for k in range(4):
        at = pl.ds(k, 2 * W, stride=SUB)
        gbuf[at, :] = gbuf[at, :] - change[:, k * LANES : (k + 1) * LANES]

    @pl.when(pos[1] == 15)
    def _():
        for h in range(2):
            gbuf[pl.ds(2 + h, 2 * W, stride=SUB), :] = b1[:, h * LANES : (h + 1) * LANES]

    @pl.when(pos[1] == 0)
    def _():
        for h in range(2):
            gbuf[pl.ds(4 + h, 2 * W, stride=SUB), :] = b0[:, h * LANES : (h + 1) * LANES]

    store = pltpu.make_async_copy(gbuf, out.at[pl.ds(2 * ROWS, 2 * ROWS)], sems.at[0])
    store.start()
    rest.wait()
    store.wait()


def corner_kernel(pos, parts, own, sent, z, out):
    row, col = pos[0], pos[1]
    out[W:] = l3231_of(parts)

    @pl.when((row == 0) & (col == 0))
    def _():
        dbar = tril(own[:W] - product_t(z[0], diag_sum(parts, 0)))
        inner = lower_half(product_t(tril(own[W:]), dbar))
        sym = product(product_t(z[0], inner), z[0])
        out[:W] = sym + sym.T

    @pl.when((row == 0) & (col == 15))
    def _():
        out[:W] = own[:W] - product_t(z[0], diag_sum(parts, 0))

    @pl.when((row == 15) & (col == 15))
    def _():
        t31 = product_t(z[0], diag_sum(parts, 0))
        out[:W] = own[:W] - product_t(z[1], diag_sum(parts, 1) - product_t(out[W:], t31))

    @pl.when(((row != 0) & (row != 15)) | ((col != 0) & (col != 15)) | ((row == 15) & (col == 0)))
    def _():
        out[:W] = sent[...]


def below_kernel(pos, smine, sother, z, out):
    @pl.when(pos[0] == 0)
    def _():
        small0, small1 = pick(pos, 1, smine[...], sother[...])
        out[...] = product(small1[:W] - product(small0[:W], small1[W:]), z[1])

    @pl.when(pos[0] != 0)
    def _():
        out[...] = jnp.zeros_like(out)


def ready_kernel(pos, sums, panels, smine, sother, b_here, z, out):
    @pl.when(pos[0] == 0)
    def _():
        sym0 = jnp.where(pos[3] == 1, sother[:W], smine[:W])
        out[...] = (
            product_t(z[0], sums[:W])
            + product(sym0, panel_row(panels, 0))
            + product(b_here[...], panel_row(panels, 1))
        )

    @pl.when(pos[0] == 15)
    def _():
        l3231 = jnp.where(pos[3] == 1, smine[W:], sother[W:])
        mix = product(z[0], product(l3231, z[1]))
        out[...] = product_t(z[1], sums[W:]) - product_t(mix, sums[:W])


def rows_kernel(pos, g, ready, panels, smine, sother, b_here, b_sent, z, done, out, gbuf, sem):
    small0, small1 = pick(pos, 1, smine[...], sother[...])

    def finished_row(first, update, corner, extra):
        load = pltpu.make_async_copy(g.at[pl.ds(first * ROWS, ROWS)], gbuf, sem)
        load.start()
        change = update()
        load.wait()
        for k in range(4):
            at = pl.ds(k, W, stride=SUB)
            gbuf[at, :] = gbuf[at, :] - change[:, k * LANES : (k + 1) * LANES]

        @pl.when(pos[1] == 15)
        def _():
            for h in range(2):
                gbuf[pl.ds(2 + h, W, stride=SUB), :] = corner[:, h * LANES : (h + 1) * LANES]

        if extra is not None:

            @pl.when(pos[1] == 0)
            def _():
                for h in range(2):
                    gbuf[pl.ds(4 + h, W, stride=SUB), :] = extra[:, h * LANES : (h + 1) * LANES]

        store = pltpu.make_async_copy(gbuf, out.at[pl.ds(first * ROWS, ROWS)], sem)
        store.start()
        store.wait()

    @pl.when(pos[0] == 0)
    def _():
        finished_row(2, lambda: ready[...], b_here[...], lower_half(small0[:W]))

    @pl.when(pos[0] == 15)
    def _():
        below = b_sent[...]
        dbar = tril(small1[:W] - product_t(below, small1[W:]))
        inner = lower_half(product_t(tril(small0[:W]), dbar))
        sym1 = product(product_t(z[1], inner), z[1])
        sym1 = sym1 + sym1.T

        def update():
            return ready[...] + product_t(below, panel_row(panels, 0)) + product(sym1, panel_row(panels, 1))

        finished_row(1, update, lower_half(sym1), None)


RING = [[(0, 7)], [(0, 2), (7, 5)], [(0, 1), (7, 6), (5, 4), (2, 3)]]


def choose_kernel(pos, moved, kept, out, *, targets):
    got = functools.reduce(jnp.logical_or, [pos[1] == t for t in targets])

    @pl.when(got)
    def _():
        out[...] = moved[...]

    @pl.when(jnp.logical_not(got))
    def _():
        out[...] = kept[...]


def tree_step(pos, value, step, weight):
    pairs = [(2 * s, 2 * t) for s, t in RING[step]]
    pairs = pairs + [(15 - s, 15 - t) for s, t in pairs]
    moved = lax.ppermute(value, "col", pairs)
    kernel = functools.partial(choose_kernel, targets=[t for _, t in pairs])
    return call(kernel, shape(*value.shape), [SMEM] + [VMEM] * 2, VMEM, [], weight, 4 * value.size)(pos, moved, value)


def flipped(value, axis, flip):
    return lax.ppermute(value, axis, [(i, i ^ flip) for i in range(lax.axis_size(axis))])


def after(value, *others):
    return lax.optimization_barrier((value, *others))[0]


def exchange(parts):
    return lax.all_to_all(parts, "row", 0, 0)


def per_device(factor, adjoint, diag_inverse):
    my_row = lax.axis_index("row")
    my_col = lax.axis_index("col")
    pos = jnp.stack([my_row, my_col, my_row // 8, my_col % 2]).astype(jnp.int32)
    g = adjoint.reshape(4 * ROWS, LANES)
    l = factor.reshape(4 * ROWS, LANES)
    z = diag_inverse
    dma = pltpu.SemaphoreType.DMA
    block = W * W * 4

    slab = call(
        entry_kernel,
        shape(2 * W, W),
        [HBM],
        VMEM,
        [pltpu.VMEM((2 * ROWS, LANES), F32), dma],
        0,
        10 * block,
        vmem=60,
    )(g)
    gmine = tree_step(pos, slab, 0, LIGHT)
    inside, fslab, piece, own = call(
        unpack_kernel,
        (shape(2 * W, 2 * W), shape(2 * W, W), shape(W, 2 * W), shape(2 * W, W)),
        [SMEM, HBM, HBM, VMEM],
        (VMEM,) * 4,
        [
            pltpu.VMEM((2 * ROWS, LANES), F32),
            pltpu.VMEM((ROWS, LANES), F32),
            pltpu.VMEM((ROWS, LANES), F32),
            dma((3,)),
        ],
        0,
        20 * block,
        vmem=50,
    )(pos, g, l, slab)
    gmine = after(gmine, fslab)
    sent = lax.ppermute(gmine, "col", [(14, 15)])
    gmine = tree_step(pos, gmine, 1, STEP_HINT)

    partial = call(
        diag_kernel, shape(16, 64, W), [SMEM] + [VMEM] * 4, VMEM, [], 8 * W**3, 12 * block
    )(pos, sent, slab, fslab, piece)
    parts = exchange(partial)
    gmine = after(gmine, partial)
    spread, chunk = call(
        first_parts_kernel,
        (shape(16, 24, 2 * W), shape(32, 2 * W)),
        [VMEM],
        (VMEM,) * 2,
        [],
        DIAG_HINT,
        10 * block,
    )(after(parts, gmine))
    gmine = tree_step(pos, gmine, 2, STEP_HINT)
    gother = flipped(after(gmine, spread), "col", 1)
    spread = exchange(spread)

    partial = call(
        sums_kernel, shape(16, 64, 2 * W), [SMEM] + [VMEM] * 4, VMEM, [], SUMS_HINT, 20 * block
    )(pos, gmine, gother, inside, chunk)

    sent = lax.ppermute(after(piece[:, W:], gmine), "col", [(15, 0)])
    smine = call(
        corner_kernel, shape(2 * W, W), [SMEM] + [VMEM] * 4, VMEM, [], CHAIN_HINT, 12 * block
    )(pos, after(spread, partial), own, sent, z)
    panels = exchange(after(partial, smine))

    for step in range(3):
        smine = tree_step(pos, smine, step, LIGHT)
    sother = flipped(smine, "col", 1)

    sums = call(
        second_parts_kernel, shape(16, 32, 2 * W), [VMEM], VMEM, [], MAIN_HINT, 8 * block
    )(panels)
    sums = exchange(sums).reshape(2 * W, 2 * W)

    out = call(
        bulk_kernel,
        shape(4 * ROWS, LANES),
        [SMEM, HBM] + [VMEM] * 6,
        HBM,
        [
            pltpu.VMEM((2 * ROWS, LANES), F32),
            pltpu.VMEM((2 * ROWS, LANES), F32),
            pltpu.VMEM((2 * W, W), F32),
            pltpu.VMEM((2 * W, W), F32),
            dma((2,)),
        ],
        30 * W**3,
        40 * block,
        vmem=57,
    )(pos, g, gmine, gother, panels, smine, sother, z)

    below_row = call(
        below_kernel, shape(W, W), [SMEM] + [VMEM] * 3, VMEM, [], 4 * W**3, 8 * block
    )(pos, smine, sother, z)
    below_sent = lax.ppermute(below_row, "row", [(0, 15)])
    ready = call(
        ready_kernel, shape(W, 2 * W), [SMEM] + [VMEM] * 6, VMEM, [], LIGHT, LIGHT
    )(pos, sums, panels, smine, sother, below_row, z)
    out = call(
        rows_kernel,
        shape(4 * ROWS, LANES),
        [SMEM, HBM] + [VMEM] * 7 + [HBM],
        HBM,
        [pltpu.VMEM((ROWS, LANES), F32), dma],
        LIGHT,
        LIGHT,
        alias={9: 0},
        vmem=57,
    )(pos, g, ready, panels, smine, sother, below_row, below_sent, z, out)
    return out.reshape(adjoint.shape)


def solution(mesh):
    placed = (P(None, "row", None, None, "col", None), P(None, "row", None, None, "col", None), P())
    return jax.shard_map(
        per_device,
        mesh=mesh,
        in_specs=placed,
        out_specs=P(None, "row", None, None, "col", None),
        check_vma=False,
    )
```

```python
import functools

import jax
import jax.numpy as jnp
from jax import lax
from jax.experimental import pallas as pl
from jax.experimental.pallas import tpu as pltpu
from jax.sharding import PartitionSpec as P

W = 256
LANES = 128
SUB = 8
ROWS = W * SUB
F32 = jnp.float32
DIAG_HINT = 20 * 10**9
MAIN_HINT = 100 * 10**9
CHAIN_HINT = 40 * 10**9
STEP_HINT = 25 * 10**9
LIGHT = 1000
SUMS_HINT = 3 * 10**8
ANY = pl.BlockSpec(memory_space=pl.ANY)
HBM = pl.BlockSpec(memory_space=pltpu.HBM)
VMEM = pl.BlockSpec(memory_space=pltpu.VMEM)
SMEM = pl.BlockSpec(memory_space=pltpu.SMEM)


def product(left, right):
    return jnp.dot(left, right, precision=lax.Precision.HIGHEST, preferred_element_type=F32)


def halves(value):
    high = value.astype(jnp.bfloat16)
    return high, (value - high.astype(F32)).astype(jnp.bfloat16)


def wide(left, right):
    (a, b), (c, d) = halves(left), halves(right)
    return sum(jnp.dot(x, y, preferred_element_type=F32) for x, y in ((a, d), (b, c), (a, c)))


def product_t(left, right):
    return lax.dot_general(
        left, right, (((0,), (0,)), ((), ())), precision=lax.Precision.HIGHEST, preferred_element_type=F32
    )


def product_nt(left, right):
    return lax.dot_general(
        left, right, (((1,), (1,)), ((), ())), precision=lax.Precision.HIGHEST, preferred_element_type=F32
    )


def masks(size):
    rows = lax.broadcasted_iota(jnp.int32, (size, size), 0)
    cols = lax.broadcasted_iota(jnp.int32, (size, size), 1)
    return rows >= cols, rows == cols


def tril(matrix):
    return jnp.where(masks(matrix.shape[0])[0], matrix, 0.0)


def lower_half(matrix):
    low, diag = masks(matrix.shape[0])
    return jnp.where(diag, 0.5 * matrix, jnp.where(low, matrix, 0.0))


def call(body, out_shape, in_specs, out_specs, scratch, flops, moved, alias=None, vmem=20):
    return pl.pallas_call(
        body,
        out_shape=out_shape,
        in_specs=in_specs,
        out_specs=out_specs,
        scratch_shapes=scratch,
        input_output_aliases=alias or {},
        compiler_params=pltpu.CompilerParams(vmem_limit_bytes=vmem * 1024 * 1024),
        cost_estimate=pl.CostEstimate(flops=flops, bytes_accessed=moved, transcendentals=0),
    )


def shape(*dims):
    return jax.ShapeDtypeStruct(dims, F32)


def piece_of(buf, first, rows, k):
    return buf[pl.ds(first * SUB + k, rows, stride=SUB), :]


def entry_kernel(g, slab, gbuf, sem):
    load = pltpu.make_async_copy(g.at[pl.ds(2 * ROWS, 2 * ROWS)], gbuf, sem)
    load.start()
    odd_col = lax.axis_index("col") % 2
    load.wait()
    for odd in range(2):

        @pl.when(odd_col == odd)
        def _():
            for h in range(2):
                slab[:, h * LANES : (h + 1) * LANES] = piece_of(gbuf, 0, 2 * W, 2 * (2 - odd) + h)


def unpack_kernel(pos, g, l, slab, inside, fslab, piece, own, lbuf, pbuf, gbuf, sems):
    odd_col = pos[3]
    first = pltpu.make_async_copy(l.at[pl.ds(2 * ROWS, 2 * ROWS)], lbuf, sems.at[0])
    first.start()
    start = pl.multiple_of((2 - pos[2]) * ROWS, ROWS)
    second = pltpu.make_async_copy(l.at[pl.ds(start, ROWS)], pbuf, sems.at[1])
    second.start()
    third = pltpu.make_async_copy(g.at[pl.ds(ROWS, ROWS)], gbuf, sems.at[2])
    third.start()
    first.wait()
    for odd in range(2):

        @pl.when(odd_col == odd)
        def _():
            for h in range(2):
                fslab[:, h * LANES : (h + 1) * LANES] = piece_of(lbuf, 0, 2 * W, 2 * (2 - odd) + h)

    for k in range(4):
        inside[:, k * LANES : (k + 1) * LANES] = piece_of(lbuf, 0, 2 * W, k)
    for h in range(2):
        own[W:, h * LANES : (h + 1) * LANES] = piece_of(lbuf, 0, W, 4 + h)
    second.wait()
    for k in range(4):
        piece[:, k * LANES : (k + 1) * LANES] = piece_of(pbuf, 0, W, k)
    third.wait()

    @pl.when(pos[0] == 15)
    def _():
        for h in range(2):
            own[:W, h * LANES : (h + 1) * LANES] = piece_of(gbuf, 0, W, 2 + h)

    @pl.when(pos[0] != 15)
    def _():
        own[:W] = slab[:W]


def pick(pos, axis, mine, other):
    odd = pos[2 + axis] == 1
    return jnp.where(odd, other, mine), jnp.where(odd, mine, other)


def live_rows(pos, value):
    rows = lax.broadcasted_iota(jnp.int32, value.shape, 0)
    return jnp.where((pos[0] == 0) & (rows < W), 0.0, value)


def diag_kernel(pos, sent, slab, fslab, piece, out):
    right = fslab[...]
    left = jnp.where(pos[3] == 1, sent[...], slab[...])
    for half, value in enumerate((left, slab[...])):
        result = product_t(live_rows(pos, value), right)
        for j in range(8):
            out[8 * half + j, :32] = result[32 * j : 32 * j + 32]
    for j in range(16):
        for h in range(2):
            out[j, 32 + 16 * h : 48 + 16 * h] = piece[16 * j : 16 * j + 16, h * W : (h + 1) * W]


def first_parts_kernel(parts, out, chunk):
    total = parts[0, :32]
    for i in range(1, 16):
        total = total + parts[i, :32]
    for h in range(2):
        lanes = slice(h * W, (h + 1) * W)
        for j in range(16):
            out[j, :16, lanes] = total[16 * h : 16 * h + 16]
            out[j, 16:, lanes] = parts[0, 48 + 8 * h : 56 + 8 * h]
        for k, source in enumerate((0, 15)):
            chunk[16 * k : 16 * k + 16, lanes] = parts[source, 32 + 16 * h : 48 + 16 * h]


def panel_row(panels, which):
    return panels[:, 32 + 16 * which : 48 + 16 * which, :].reshape(W, 2 * W)


def diag_sum(parts, half):
    return jnp.concatenate(
        [parts[8 * half + j, :16, h * W : (h + 1) * W] for j in range(8) for h in range(2)], axis=0
    )


def l3231_of(parts):
    return jnp.concatenate(
        [parts[j, 16:, h * W : (h + 1) * W] for j in range(16) for h in range(2)], axis=0
    )


def sums_kernel(pos, mine, other, inside, chunk, out):
    right = inside[...]
    for half, value in enumerate(pick(pos, 1, mine[...], other[...])):
        result = product_t(live_rows(pos, value), right)
        for j in range(8):
            out[8 * half + j, :32] = result[32 * j : 32 * j + 32]
    for j in range(16):
        out[j, 32:] = chunk[...]


def second_parts_kernel(parts, out):
    total = parts[0, :32]
    for i in range(1, 16):
        total = total + parts[i, :32]
    for i in range(16):
        out[i] = total


def bulk_kernel(pos, g, gmine, gother, panels, smine, sother, z, out, gbuf, abuf, b0, b1, sems):
    load = pltpu.make_async_copy(g.at[pl.ds(2 * ROWS, 2 * ROWS)], gbuf, sems.at[0])
    load.start()
    above = pltpu.make_async_copy(g.at[pl.ds(0, 2 * ROWS)], abuf, sems.at[1])
    above.start()
    g32, g31 = pick(pos, 1, gmine[...], gother[...])
    l3231 = jnp.where(pos[3] == 1, smine[W:], sother[W:])
    below0 = product(g32, z[0])
    b0[...] = below0
    below1 = product(g31 - product(below0, l3231), z[1])
    b1[...] = below1
    change = wide(below0, panel_row(panels, 0)) + wide(below1, panel_row(panels, 1))
    above.wait()
    rest = pltpu.make_async_copy(abuf, out.at[pl.ds(0, 2 * ROWS)], sems.at[1])
    rest.start()
    load.wait()
    for k in range(4):
        at = pl.ds(k, 2 * W, stride=SUB)
        gbuf[at, :] = gbuf[at, :] - change[:, k * LANES : (k + 1) * LANES]

    @pl.when(pos[1] == 15)
    def _():
        for h in range(2):
            gbuf[pl.ds(2 + h, 2 * W, stride=SUB), :] = b1[:, h * LANES : (h + 1) * LANES]

    @pl.when(pos[1] == 0)
    def _():
        for h in range(2):
            gbuf[pl.ds(4 + h, 2 * W, stride=SUB), :] = b0[:, h * LANES : (h + 1) * LANES]

    store = pltpu.make_async_copy(gbuf, out.at[pl.ds(2 * ROWS, 2 * ROWS)], sems.at[0])
    store.start()
    rest.wait()
    store.wait()


def corner_kernel(pos, parts, own, sent, z, out):
    row, col = pos[0], pos[1]
    out[W:] = l3231_of(parts)

    @pl.when((row == 0) & (col == 0))
    def _():
        dbar = tril(own[:W] - product_t(z[0], diag_sum(parts, 0)))
        inner = lower_half(product_t(tril(own[W:]), dbar))
        sym = product(product_t(z[0], inner), z[0])
        out[:W] = sym + sym.T

    @pl.when((row == 0) & (col == 15))
    def _():
        out[:W] = own[:W] - product_t(z[0], diag_sum(parts, 0))

    @pl.when((row == 15) & (col == 15))
    def _():
        t31 = product_t(z[0], diag_sum(parts, 0))
        out[:W] = own[:W] - product_t(z[1], diag_sum(parts, 1) - product_t(out[W:], t31))

    @pl.when(((row != 0) & (row != 15)) | ((col != 0) & (col != 15)) | ((row == 15) & (col == 0)))
    def _():
        out[:W] = sent[...]


def below_kernel(pos, smine, sother, z, out):
    @pl.when(pos[0] == 0)
    def _():
        small0, small1 = pick(pos, 1, smine[...], sother[...])
        out[...] = product(small1[:W] - product(small0[:W], small1[W:]), z[1])

    @pl.when(pos[0] != 0)
    def _():
        out[...] = jnp.zeros_like(out)


def ready_kernel(pos, sums, panels, smine, sother, b_here, z, out):
    @pl.when(pos[0] == 0)
    def _():
        sym0 = jnp.where(pos[3] == 1, sother[:W], smine[:W])
        out[...] = (
            product_t(z[0], sums[:W])
            + product(sym0, panel_row(panels, 0))
            + product(b_here[...], panel_row(panels, 1))
        )

    @pl.when(pos[0] == 15)
    def _():
        l3231 = jnp.where(pos[3] == 1, smine[W:], sother[W:])
        mix = product(z[0], product(l3231, z[1]))
        out[...] = product_t(z[1], sums[W:]) - product_t(mix, sums[:W])


def rows_kernel(pos, g, ready, panels, smine, sother, b_here, b_sent, z, done, out, gbuf, sem):
    small0, small1 = pick(pos, 1, smine[...], sother[...])

    def finished_row(first, update, corner, extra):
        load = pltpu.make_async_copy(g.at[pl.ds(first * ROWS, ROWS)], gbuf, sem)
        load.start()
        change = update()
        load.wait()
        for k in range(4):
            at = pl.ds(k, W, stride=SUB)
            gbuf[at, :] = gbuf[at, :] - change[:, k * LANES : (k + 1) * LANES]

        @pl.when(pos[1] == 15)
        def _():
            for h in range(2):
                gbuf[pl.ds(2 + h, W, stride=SUB), :] = corner[:, h * LANES : (h + 1) * LANES]

        if extra is not None:

            @pl.when(pos[1] == 0)
            def _():
                for h in range(2):
                    gbuf[pl.ds(4 + h, W, stride=SUB), :] = extra[:, h * LANES : (h + 1) * LANES]

        store = pltpu.make_async_copy(gbuf, out.at[pl.ds(first * ROWS, ROWS)], sem)
        store.start()
        store.wait()

    @pl.when(pos[0] == 0)
    def _():
        finished_row(2, lambda: ready[...], b_here[...], lower_half(small0[:W]))

    @pl.when(pos[0] == 15)
    def _():
        below = b_sent[...]
        dbar = tril(small1[:W] - product_t(below, small1[W:]))
        inner = lower_half(product_t(tril(small0[:W]), dbar))
        sym1 = product(product_t(z[1], inner), z[1])
        sym1 = sym1 + sym1.T

        def update():
            return ready[...] + product_t(below, panel_row(panels, 0)) + product(sym1, panel_row(panels, 1))

        finished_row(1, update, lower_half(sym1), None)


RING = [[(0, 7)], [(0, 2), (7, 5)], [(0, 1), (7, 6), (5, 4), (2, 3)]]


def choose_kernel(pos, moved, kept, out, *, targets):
    got = functools.reduce(jnp.logical_or, [pos[1] == t for t in targets])

    @pl.when(got)
    def _():
        out[...] = moved[...]

    @pl.when(jnp.logical_not(got))
    def _():
        out[...] = kept[...]


def tree_step(pos, value, step, weight):
    pairs = [(2 * s, 2 * t) for s, t in RING[step]]
    pairs = pairs + [(15 - s, 15 - t) for s, t in pairs]
    moved = lax.ppermute(value, "col", pairs)
    kernel = functools.partial(choose_kernel, targets=[t for _, t in pairs])
    return call(kernel, shape(*value.shape), [SMEM] + [VMEM] * 2, VMEM, [], weight, 4 * value.size)(pos, moved, value)


def flipped(value, axis, flip):
    return lax.ppermute(value, axis, [(i, i ^ flip) for i in range(lax.axis_size(axis))])


def after(value, *others):
    return lax.optimization_barrier((value, *others))[0]


def exchange(parts):
    return lax.all_to_all(parts, "row", 0, 0)


def per_device(factor, adjoint, diag_inverse):
    my_row = lax.axis_index("row")
    my_col = lax.axis_index("col")
    pos = jnp.stack([my_row, my_col, my_row // 8, my_col % 2]).astype(jnp.int32)
    g = adjoint.reshape(4 * ROWS, LANES)
    l = factor.reshape(4 * ROWS, LANES)
    z = diag_inverse
    dma = pltpu.SemaphoreType.DMA
    block = W * W * 4

    slab = call(
        entry_kernel,
        shape(2 * W, W),
        [HBM],
        VMEM,
        [pltpu.VMEM((2 * ROWS, LANES), F32), dma],
        0,
        10 * block,
        vmem=60,
    )(g)
    gmine = tree_step(pos, slab, 0, LIGHT)
    inside, fslab, piece, own = call(
        unpack_kernel,
        (shape(2 * W, 2 * W), shape(2 * W, W), shape(W, 2 * W), shape(2 * W, W)),
        [SMEM, HBM, HBM, VMEM],
        (VMEM,) * 4,
        [
            pltpu.VMEM((2 * ROWS, LANES), F32),
            pltpu.VMEM((ROWS, LANES), F32),
            pltpu.VMEM((ROWS, LANES), F32),
            dma((3,)),
        ],
        0,
        20 * block,
        vmem=50,
    )(pos, g, l, slab)
    gmine = after(gmine, fslab)
    sent = lax.ppermute(gmine, "col", [(14, 15)])
    gmine = tree_step(pos, gmine, 1, STEP_HINT)

    partial = call(
        diag_kernel, shape(16, 64, W), [SMEM] + [VMEM] * 4, VMEM, [], 8 * W**3, 12 * block
    )(pos, sent, slab, fslab, piece)
    parts = exchange(partial)
    gmine = after(gmine, partial)
    spread, chunk = call(
        first_parts_kernel,
        (shape(16, 24, 2 * W), shape(32, 2 * W)),
        [VMEM],
        (VMEM,) * 2,
        [],
        DIAG_HINT,
        10 * block,
    )(after(parts, gmine))
    gmine = tree_step(pos, gmine, 2, STEP_HINT)
    gother = flipped(after(gmine, spread), "col", 1)
    spread = exchange(spread)

    partial = call(
        sums_kernel, shape(16, 64, 2 * W), [SMEM] + [VMEM] * 4, VMEM, [], SUMS_HINT, 20 * block
    )(pos, gmine, gother, inside, chunk)

    sent = lax.ppermute(after(piece[:, W:], gmine), "col", [(15, 0)])
    smine = call(
        corner_kernel, shape(2 * W, W), [SMEM] + [VMEM] * 4, VMEM, [], CHAIN_HINT, 12 * block
    )(pos, after(spread, partial), own, sent, z)
    panels = exchange(after(partial, smine))

    for step in range(3):
        smine = tree_step(pos, smine, step, LIGHT)
    sother = flipped(smine, "col", 1)

    sums = call(
        second_parts_kernel, shape(16, 32, 2 * W), [VMEM], VMEM, [], MAIN_HINT, 8 * block
    )(panels)
    sums = exchange(sums).reshape(2 * W, 2 * W)

    out = call(
        bulk_kernel,
        shape(4 * ROWS, LANES),
        [SMEM, HBM] + [VMEM] * 6,
        HBM,
        [
            pltpu.VMEM((2 * ROWS, LANES), F32),
            pltpu.VMEM((2 * ROWS, LANES), F32),
            pltpu.VMEM((2 * W, W), F32),
            pltpu.VMEM((2 * W, W), F32),
            dma((2,)),
        ],
        30 * W**3,
        40 * block,
        vmem=57,
    )(pos, g, gmine, gother, panels, smine, sother, z)

    below_row = call(
        below_kernel, shape(W, W), [SMEM] + [VMEM] * 3, VMEM, [], 4 * W**3, 8 * block
    )(pos, smine, sother, z)
    below_sent = lax.ppermute(below_row, "row", [(0, 15)])
    ready = call(
        ready_kernel, shape(W, 2 * W), [SMEM] + [VMEM] * 6, VMEM, [], LIGHT, LIGHT
    )(pos, sums, panels, smine, sother, below_row, z)
    out = call(
        rows_kernel,
        shape(4 * ROWS, LANES),
        [SMEM, HBM] + [VMEM] * 7 + [HBM],
        HBM,
        [pltpu.VMEM((ROWS, LANES), F32), dma],
        LIGHT,
        LIGHT,
        alias={9: 0},
        vmem=57,
    )(pos, g, ready, panels, smine, sother, below_row, below_sent, z, out)
    return out.reshape(adjoint.shape)


def solution(mesh):
    placed = (P(None, "row", None, None, "col", None), P(None, "row", None, None, "col", None), P())
    return jax.shard_map(
        per_device,
        mesh=mesh,
        in_specs=placed,
        out_specs=P(None, "row", None, None, "col", None),
        check_vma=False,
    )
```
